32 devices in a mesh: groups: 2 (over y), member: 4 (over x, core), grid: 4 (over z).
Axes of the slice: x: 2, y: 2, z: 4, core: 2. Of those that a mesh axis runs over, the one named last changes fastest.
Arguments:
- latent: bfloat16 [8, 256, 1024], P(('groups', 'member'), 'grid'), parts along dimension 0, may hold values from -6 to 6
- w_message: bfloat16 [1024, 1024], replicated, may hold values from -0.1875 to 0.1875
- edge_embed: float32 [4, 1024], replicated, may hold values from -3 to 3
- w_node: bfloat16 [1024, 1024], replicated, may hold values from -0.1875 to 0.1875
- w_output: bfloat16 [100, 1024], replicated, may hold values from -0.1875 to 0.1875
- send_list: int32 [4, 4, 8], P('grid'), may hold values from 0 to 63, as said below
- edge_src: int32 [3, 4096], P(None, 'grid'), may hold values from 0 to 31, as said below
- edge_feat: float32 [4, 3, 4096], P(None, None, 'grid'), may hold values from -6 to 6
- cell_area: float32 [4096], P('grid'), may hold values from 0.3 to 3
- target: bfloat16 [100, 8192], P(None, ('groups', 'grid')), parts along dimension 1, may hold values from -6 to 6
Outputs:
- latent_grad: bfloat16 [8, 256, 1024], P(('groups', 'member'), 'grid'), parts along dimension 0
- point_score: float32 [8192], P(('groups', 'grid')), parts along dimension 0
The draws below stay inside these ranges and needn't reach their ends.
There are 2 independent parts, one for each index of `groups`. The reference program is written for one: setup_inputs(seed, part) draws one part's arguments, and reference() takes and returns one part's arrays. A program takes and returns all parts, laid end to end along the dimension named above; an argument that names none is the same for every part. Nothing has to cross between parts.
Inputs may be any that keep to these rules, and one draw needn't show every extreme that they name: send_list[s, b, j] is a row among the 64 mesh nodes owned by block s; entries may repeat. edge_src[k, g] = s * 8 + j names slot j of the rows that owner s sends to the block holding grid point g.
All inputs are finite; a program needn't handle non-finite values.
Results may differ from the reference program's by a relative error of at most 0.0062.
Values may be sent and summed in bfloat16 or wider, within the bound.
A program may use at most 64 MiB of HBM per device.

```python
import math
import jax
import jax.numpy as jnp
from jax import lax

D = 1024
VARS = 100
GRID_DEV = 1024
MESH_DEV = 64
SLOTS = 8
K = 3
EF = 4
MEMBERS = 4
NGRID = 4096
MESH = 256


def live_counts(key, owners):
    counts = jax.random.randint(key, (owners, owners), 1, SLOTS + 1)
    return jnp.where(jnp.eye(owners, dtype=bool), SLOTS, counts)


def draw_send_list(key, part):
    key = jax.random.fold_in(key, 3)
    owners = MESH // MESH_DEV
    chosen = jax.random.randint(key, (owners, owners, SLOTS), 0, MESH_DEV)
    diagonal = jnp.eye(owners, dtype=bool)[:, :, None]
    position = jnp.arange(SLOTS)[None, None, :]
    chosen = jnp.where(diagonal & (position == 0), MESH_DEV - 1, chosen)
    chosen = jnp.where(diagonal & (position == 1), 0, chosen)
    return chosen.astype(jnp.int32)


def draw_edge_src(key, part):
    owners = MESH // MESH_DEV
    counts = live_counts(jax.random.fold_in(key, 5), owners)
    key = jax.random.fold_in(key, 7)
    key_source, key_slot = jax.random.split(key)
    source = jax.random.randint(key_source, (K, NGRID), 0, owners)
    block_of = jnp.broadcast_to((jnp.arange(NGRID) // GRID_DEV)[None, :], (K, NGRID))
    live = counts[source, block_of]
    fraction = jax.random.randint(key_slot, (K, NGRID), 0, 1 << 20)
    slot_pick = fraction * live // (1 << 20)
    chosen = source * SLOTS + slot_pick
    first_point = (jnp.arange(NGRID) % GRID_DEV == 0)[None, :]
    which_edge = jnp.arange(K)[:, None]
    chosen = jnp.where(first_point & (which_edge == 0), block_of * SLOTS + SLOTS - 1, chosen)
    chosen = jnp.where(first_point & (which_edge == 1), 0, chosen)
    return chosen.astype(jnp.int32)


def steps_of(rng, shape, cuts, low, top_value):
    def one(dim, shards_of):
        draws = jax.random.uniform(jax.random.fold_in(jax.random.fold_in(rng, 6), dim), (shards_of,), jnp.float32, low / len(cuts), top_value / len(cuts))
        return jnp.repeat(jnp.exp(draws), shape[dim] // shards_of).reshape((-1,) + (1,) * (len(shape) - dim - 1))

    level = one(*cuts[0])
    for cut in cuts[1:]:
        level = level * one(*cut)
    return level


def bell_draw(key, shape, width, bound, cuts=(), held_as=jnp.bfloat16):
    level = steps_of(key, shape, cuts, -0.22, 0.18) if cuts else 1.0
    result = jax.random.normal(key, shape, jnp.float32) * width * level
    return jnp.minimum(jnp.maximum(result, -bound), bound).astype(held_as)


def setup_inputs(seed: int = 0, part: int = 0) -> dict:
    key_list = jax.random.split(jax.random.key(seed), 11)
    own_keys = jax.random.split(jax.random.fold_in(key_list[10], part), 11)
    latent = bell_draw(own_keys[0], (MEMBERS, MESH, D), 1.0, 6.0, ((0, 4), (1, 4)))
    w_message = bell_draw(key_list[1], (D, D), D ** -0.5, 0.1875)
    edge_embed = bell_draw(key_list[2], (EF, D), EF ** -0.5, 3.0, (), jnp.float32)
    w_node = bell_draw(key_list[3], (D, D), D ** -0.5, 0.1875)
    w_output = bell_draw(key_list[4], (VARS, D), D ** -0.5, 0.1875)
    send_list = draw_send_list(jax.random.fold_in(key_list[10], 71), part)
    edge_src = draw_edge_src(jax.random.fold_in(key_list[10], 71), part)
    edge_feat = bell_draw(key_list[7], (EF, K, NGRID), 1.0, 6.0, ((2, 4),), jnp.float32)
    cell_area = jnp.clip(jnp.exp(math.log(3.0) - 2.3025851 * jax.random.uniform(key_list[8], (NGRID,), jnp.float32) ** steps_of(key_list[8], (NGRID,), ((0, 4),), -0.2, 0.2)), 0.3, 3.0)
    target = bell_draw(own_keys[9], (VARS, NGRID), 1.0, 6.0, ((1, 4),))
    return dict(latent=latent, w_message=w_message, edge_embed=edge_embed, w_node=w_node, w_output=w_output, send_list=send_list, edge_src=edge_src, edge_feat=edge_feat, cell_area=cell_area, target=target)


softness = 0.1

def silu_slope(value):
    sigma = jax.nn.sigmoid(value)
    return sigma * (1.0 + value * (1.0 - sigma))

def smooth_abs(value):
    return jnp.sqrt(value * value + softness * softness)

def smooth_slope(value):
    return value / smooth_abs(value)

def edge_terms(features, edge_embed, which):
    total = features[0, which, :][:, None] * edge_embed[0][None, :]
    for feature in range(1, features.shape[0]):
        total = total + features[feature, which, :][:, None] * edge_embed[feature][None, :]
    return total

def gather_rows(projected, send_list, block_id):
    owners = send_list.shape[0]
    starts = jnp.arange(owners, dtype=jnp.int32)[:, None] * MESH_DEV
    picked = starts + send_list[:, block_id, :]
    return (jnp.take(projected, picked.reshape(-1), axis=0), picked.reshape(-1))

def decode_forward(received, sources, features, edge_embed, w_node, w_output):
    summed = jnp.zeros((sources.shape[1], received.shape[1]), jnp.float32)
    for edge in range(K):
        pre_act = jnp.take(received, sources[edge], axis=0).astype(jnp.float32) + edge_terms(features, edge_embed, edge)
        summed = summed + jax.nn.silu(pre_act)
    hidden = (summed / K).astype(jnp.bfloat16)
    mixed = jnp.dot(hidden, w_node, preferred_element_type=jnp.float32)
    outer = (hidden.astype(jnp.float32) + jax.nn.silu(mixed)).astype(jnp.bfloat16)
    predicted = jnp.dot(w_output, outer.T, preferred_element_type=jnp.float32).astype(jnp.bfloat16)
    return (predicted, mixed)

def decode_backward(received, sources, features, edge_embed, w_node, w_output, mixed, grad_pred):
    grad_outer = jnp.dot(grad_pred.T, w_output, preferred_element_type=jnp.float32)
    grad_mixed = (grad_outer * silu_slope(mixed)).astype(jnp.bfloat16)
    grad_hidden = grad_outer + jnp.dot(grad_mixed, w_node.T, preferred_element_type=jnp.float32)
    grad_summed = grad_hidden / K
    slot_grad = jnp.zeros(received.shape, jnp.float32)
    for edge in range(K):
        pre_act = jnp.take(received, sources[edge], axis=0).astype(jnp.float32) + edge_terms(features, edge_embed, edge)
        edge_grad = lax.optimization_barrier((grad_summed * silu_slope(pre_act)).astype(jnp.bfloat16))
        slot_grad = slot_grad + jax.ops.segment_sum(edge_grad.astype(jnp.float32), sources[edge], num_segments=received.shape[0])
    return slot_grad

def score_terms(ensemble, truth, cell_area):
    members = ensemble.shape[0]
    skill = jnp.zeros(truth.shape, jnp.float32)
    spread = jnp.zeros(truth.shape, jnp.float32)
    for member in range(members):
        skill = skill + smooth_abs(ensemble[member] - truth)
        spread = spread + lax.optimization_barrier(jnp.sum(smooth_abs(ensemble[member][None] - ensemble), axis=0))
    spread = spread - members * softness
    crps = skill / members - spread / (2.0 * members * (members - 1))
    return cell_area * lax.optimization_barrier(jnp.mean(crps, axis=0))

def slope_terms(own, ensemble, truth, cell_area):
    members = ensemble.shape[0]
    pairs = jnp.zeros(own.shape, jnp.float32)
    for member in range(members):
        pairs = pairs + smooth_slope(own - ensemble[member])
    return cell_area * (smooth_slope(own - truth) / members - pairs / (members * (members - 1)))

def reference(latent, w_message, edge_embed, w_node, w_output, send_list, edge_src, edge_feat, cell_area, target):
    owners = send_list.shape[0]
    projected = lax.map(lambda mesh_rows: jnp.dot(mesh_rows, w_message, preferred_element_type=jnp.float32).astype(jnp.bfloat16), latent)

    def block_inputs(step_id):
        member = step_id // owners
        block_id = step_id % owners
        received, picked = gather_rows(projected[member], send_list, block_id)
        sources = lax.dynamic_slice_in_dim(edge_src, (block_id * GRID_DEV).astype(jnp.int32), GRID_DEV, 1)
        features = lax.dynamic_slice_in_dim(edge_feat, (block_id * GRID_DEV).astype(jnp.int32), GRID_DEV, 2)
        return (member, block_id, received, picked, sources, features)

    def forward_step(step_id):
        member, block_id, received, picked, sources, features = block_inputs(step_id)
        return decode_forward(received, sources, features, edge_embed, w_node, w_output)
    step_ids = jnp.arange(MEMBERS * owners, dtype=jnp.int32)
    predicted, mixed_all = lax.map(forward_step, step_ids)
    ensemble = predicted.reshape(MEMBERS, owners, VARS, GRID_DEV).transpose(0, 2, 1, 3).reshape(MEMBERS, VARS, NGRID).astype(jnp.float32)
    truth = target.astype(jnp.float32)
    point_score = score_terms(ensemble, truth, cell_area)
    grad_pred = slope_terms(ensemble, ensemble, truth, cell_area).astype(jnp.bfloat16)

    def backward_step(rows_grad, step_id):
        member, block_id, received, picked, sources, features = block_inputs(step_id)
        grad_block = lax.dynamic_slice_in_dim(grad_pred[member], (block_id * GRID_DEV).astype(jnp.int32), GRID_DEV, 1)
        slot_grad = decode_backward(received, sources, features, edge_embed, w_node, w_output, mixed_all[step_id], grad_block)
        slot_low = lax.optimization_barrier(slot_grad.astype(jnp.bfloat16))
        return (rows_grad.at[member, picked].add(slot_low.astype(jnp.float32)), step_id)
    rows_grad, unused = lax.scan(backward_step, jnp.zeros((MEMBERS, MESH, D), jnp.float32), step_ids)
    latent_grad = lax.map(lambda grads: jnp.dot(grads.astype(jnp.bfloat16), w_message.T, preferred_element_type=jnp.float32).astype(jnp.bfloat16), rows_grad)
    return (latent_grad, point_score)
```

```python
import functools

import jax
import jax.numpy as jnp
from jax import lax
from jax.experimental import pallas as pl
from jax.experimental.pallas import tpu as pltpu
from jax.sharding import PartitionSpec as P

F32 = jnp.float32
BF16 = jnp.bfloat16
MESH = pl.DeviceIdType.MESH

softness = 0.1
CHUNK = 256
TILE = 256


def rup(value, unit):
    return (value + unit - 1) // unit * unit


def nt_dot(a, b):
    return lax.dot_general(a, b, (((1,), (1,)), ((), ())), preferred_element_type=F32)


def tn_dot(a, b):
    return lax.dot_general(a, b, (((0,), (0,)), ((), ())), preferred_element_type=F32)


def nn_dot(a, b):
    return jnp.dot(a, b, preferred_element_type=F32)


def kernel(
    members,
    owners,
    latent_ref,
    wm_hbm,
    embed_ref,
    wn_hbm,
    wo_ref,
    sends_ref,
    src_ref,
    feat_ref,
    area_ref,
    target_ref,
    grad_ref,
    score_ref,
    wm,
    wn,
    table,
    outgoing,
    received,
    back,
    returned,
    picks,
    picks_t,
    terms,
    low,
    hid,
    outr,
    edge_slope,
    mix_slope,
    go_scr,
    gm_scr,
    ens,
    slot,
    local_sem,
    out_send,
    out_recv,
    back_send,
    back_recv,
    cross_send,
    cross_recv,
    sib_send,
    sib_recv,
):
    width = latent_ref.shape[2]
    nodes = latent_ref.shape[1]
    edges, points = src_ref.shape
    feats = feat_ref.shape[0]
    slots = sends_ref.shape[2]
    variables = wo_ref.shape[0]
    rows_in = owners * slots
    chunks = points // CHUNK
    tiles = [slice(t, t + TILE) for t in range(0, width, TILE)]
    pairs = members // 2

    zi = lax.axis_index("grid")
    mi = lax.axis_index("member")
    hi, lo = lax.div(mi, 2), lax.rem(mi, 2)
    sibling = hi * 2 + 1 - lo

    load_wm = pltpu.make_async_copy(wm_hbm, wm, local_sem.at[0])
    load_wn = pltpu.make_async_copy(wn_hbm, wn, local_sem.at[1])
    load_wm.start()
    load_wn.start()

    def grid_peer(step):
        return lax.rem(zi + step, owners)

    def member_peer(step):
        return lax.rem(hi + step, pairs) * 2 + lo

    barrier = pltpu.get_barrier_semaphore()
    for step in range(1, owners):
        pl.semaphore_signal(
            barrier, inc=1, device_id={"grid": grid_peer(step)}, device_id_type=MESH
        )
    for step in range(1, pairs):
        pl.semaphore_signal(
            barrier, inc=1, device_id={"member": member_peer(step)}, device_id_type=MESH
        )
    pl.semaphore_signal(barrier, inc=1, device_id={"member": sibling}, device_id_type=MESH)

    eye = lax.broadcasted_iota(jnp.int32, (slots, slots), 0) == lax.broadcasted_iota(
        jnp.int32, (slots, slots), 1
    )
    node_id = lax.broadcasted_iota(jnp.int32, (slots, nodes), 1).astype(F32)
    for block in range(owners):
        line = jnp.broadcast_to(sends_ref[0, block : block + 1, :].astype(F32), (slots, slots))
        column = jnp.sum(jnp.where(eye, line, 0.0), axis=1, keepdims=True)
        table[block * slots : (block + 1) * slots, :] = jnp.where(column == node_id, 1.0, 0.0)

    load_wm.wait()
    chosen = nn_dot(table[...].astype(BF16), latent_ref[0]).astype(BF16)
    projected = nn_dot(chosen, wm[...]).astype(BF16).astype(F32)
    outgoing[...] = projected.reshape(owners, slots, width)

    pl.semaphore_wait(barrier, owners - 1 + pairs - 1 + 1)

    def out_copy(step):
        return pltpu.make_async_remote_copy(
            src_ref=outgoing.at[grid_peer(step)],
            dst_ref=received.at[zi],
            send_sem=out_send.at[step],
            recv_sem=out_recv.at[step],
            device_id={"grid": grid_peer(step)},
            device_id_type=MESH,
        )

    def out_arrival(step):
        origin = lax.rem(zi + owners - step, owners)
        return pltpu.make_async_remote_copy(
            src_ref=outgoing.at[origin],
            dst_ref=received.at[origin],
            send_sem=out_send.at[step],
            recv_sem=out_recv.at[step],
            device_id={"grid": origin},
            device_id_type=MESH,
        )

    for step in range(owners - 1, 0, -1):
        out_copy(step).start()
    received[zi] = outgoing[zi]

    depth = terms.shape[0]
    for edge in range(edges):
        slot_id = lax.broadcasted_iota(jnp.int32, (rows_in, points), 0)
        hot = jnp.where(slot_id == src_ref[edge : edge + 1, :], 1.0, 0.0)
        picks[edge] = hot.astype(BF16)
        value = feat_ref[:, edge, :]
        high = value.astype(BF16).astype(F32)
        rest = value - high
        parts = [hot, high, rest, high, rest]
        parts.append(jnp.zeros((depth - rows_in - 4 * feats, points), F32))
        picks_t[edge] = jnp.concatenate(parts, axis=0).T.astype(BF16)
    embed = embed_ref[...] * 0.5
    high = embed.astype(BF16).astype(F32)
    rest = embed - high
    tail = [high, high, rest, rest]
    tail.append(jnp.zeros((depth - rows_in - 4 * feats, width), F32))
    terms[rows_in:, :] = jnp.concatenate(tail, axis=0).astype(BF16)
    ens[mi] = jnp.zeros(ens.shape[1:], BF16)
    slot[...] = jnp.zeros(slot.shape, F32)

    for step in range(1, owners):
        out_arrival(step).wait_recv()
    terms[:rows_in, :] = (received[...].reshape(rows_in, width) * 0.5).astype(BF16)
    load_wn.wait()

    def cross_copy(step, c):
        return pltpu.make_async_remote_copy(
            src_ref=ens.at[mi, c],
            dst_ref=ens.at[mi, c],
            send_sem=cross_send.at[step, c],
            recv_sem=cross_recv.at[step, c],
            device_id={"member": member_peer(step)},
            device_id_type=MESH,
        )

    def origin_of(step, side):
        return lax.rem(hi + pairs - step, pairs) * 2 + side

    def cross_arrival(step, c):
        origin = origin_of(step, lo)
        return pltpu.make_async_remote_copy(
            src_ref=ens.at[origin, c],
            dst_ref=ens.at[origin, c],
            send_sem=cross_send.at[step, c],
            recv_sem=cross_recv.at[step, c],
            device_id={"member": origin},
            device_id_type=MESH,
        )

    def sib_copy(step, c, side):
        held = ens.at[origin_of(step, side), c]
        return pltpu.make_async_remote_copy(
            src_ref=held,
            dst_ref=held,
            send_sem=sib_send.at[step, c],
            recv_sem=sib_recv.at[step, c],
            device_id={"member": sibling},
            device_id_type=MESH,
        )

    def pass_on(c):
        for step in range(1, pairs):
            cross_arrival(step, c).wait_recv()
            sib_copy(step, c, lo).start()

    def forward(c, carry):
        span = pl.ds(pl.multiple_of(c * CHUNK, CHUNK), CHUNK)
        for tile in tiles:
            total = None
            for edge in range(edges):
                half = nn_dot(picks_t[edge, span, :], terms[:, tile])
                th = jnp.tanh(half)
                bent = half * th
                act = half + bent
                total = act if total is None else total + act
                edge_slope[edge, span, tile] = ((th + 1.0) + (half - bent * th)).astype(BF16)
            hid[:, tile] = (total * (1.0 / edges)).astype(BF16)
        for tile in tiles:
            half = nn_dot(hid[...], wn[:, tile]) * 0.5
            th = jnp.tanh(half)
            bent = half * th
            mix_slope[span, tile] = ((th + 1.0) + (half - bent * th)) * 0.5
            outr[:, tile] = (hid[:, tile].astype(F32) + (half + bent)).astype(BF16)
        ens[mi, c, :variables, :] = nt_dot(wo_ref[...], outr[...]).astype(BF16)
        for step in range(1, pairs):
            cross_copy(step, c).start()
        sib_copy(0, c, lo).start()

        @pl.when(c > 0)
        def _():
            pass_on(c - 1)

        return carry

    lax.fori_loop(0, chunks, forward, 0)

    eps = softness * softness

    def backward(c, carry):
        span = pl.ds(pl.multiple_of(c * CHUNK, CHUNK), CHUNK)
        for step in range(pairs):
            sib_copy(step, c, 1 - lo).wait_recv()
        own = ens[mi, c, :variables, :].astype(F32)
        spread = jnp.zeros(own.shape, F32)
        for member in range(members):
            gap = own - ens[member, c, :variables, :].astype(F32)
            spread = spread + gap * lax.rsqrt(gap * gap + eps)
        gap = own - target_ref[:, span].astype(F32)
        slope = gap * lax.rsqrt(gap * gap + eps) * (1.0 / members) - spread * (
            1.0 / (members * (members - 1))
        )
        gp = (area_ref[:, span] * slope).astype(BF16)
        for tile in tiles:
            go = tn_dot(gp, wo_ref[:, tile])
            go_scr[:, tile] = go
            gm_scr[:, tile] = (go * mix_slope[span, tile]).astype(BF16)
        for tile in tiles:
            gh = go_scr[:, tile] + nt_dot(gm_scr[...], wn[tile, :])
            gh = gh * (0.5 / edges)
            add = None
            for edge in range(edges):
                eg = (gh * edge_slope[edge, span, tile].astype(F32)).astype(BF16)
                part = nn_dot(picks[edge, :, span], eg)
                add = part if add is None else add + part
            slot[:, tile] += add

        @pl.when(c == 0)
        def _():
            pass_on(chunks - 1)

        return carry

    lax.fori_loop(0, chunks, backward, 0)

    back[...] = slot[...].astype(BF16).astype(F32).reshape(owners, slots, width)

    def back_copy(step):
        return pltpu.make_async_remote_copy(
            src_ref=back.at[grid_peer(step)],
            dst_ref=returned.at[zi],
            send_sem=back_send.at[step],
            recv_sem=back_recv.at[step],
            device_id={"grid": grid_peer(step)},
            device_id_type=MESH,
        )

    def back_arrival(step):
        origin = lax.rem(zi + owners - step, owners)
        return pltpu.make_async_remote_copy(
            src_ref=back.at[origin],
            dst_ref=returned.at[origin],
            send_sem=back_send.at[step],
            recv_sem=back_recv.at[step],
            device_id={"grid": origin},
            device_id_type=MESH,
        )

    for step in range(owners - 1, 0, -1):
        back_copy(step).start()
    returned[zi] = back[zi]

    def score(c, carry):
        span = pl.ds(pl.multiple_of(c * CHUNK, CHUNK), CHUNK)
        truth = target_ref[:, span].astype(F32)
        values = [ens[member, c, :variables, :].astype(F32) for member in range(members)]
        skill = jnp.zeros(truth.shape, F32)
        spread = jnp.zeros(truth.shape, F32)
        for a in range(members):
            gap = values[a] - truth
            skill = skill + jnp.sqrt(gap * gap + eps)
            for b in range(a):
                gap = values[a] - values[b]
                spread = spread + jnp.sqrt(gap * gap + eps)
        crps = skill * (1.0 / members) - spread * (1.0 / (members * (members - 1)))
        mean = jnp.sum(crps, axis=0, keepdims=True) * (1.0 / variables)
        score_ref[:, span] = area_ref[:, span] * mean
        return carry

    lax.fori_loop(0, chunks, score, 0)

    for step in range(1, owners):
        back_arrival(step).wait_recv()
    gathered = returned[...].reshape(rows_in, width).astype(BF16)
    row_grad = tn_dot(table[...].astype(BF16), gathered).astype(BF16)
    grad_ref[0] = nt_dot(row_grad, wm[...]).astype(BF16)

    for step in range(1, owners):
        out_copy(step).wait_send()
        back_copy(step).wait_send()

    def drain(c, carry):
        for step in range(1, pairs):
            cross_copy(step, c).wait_send()
        for step in range(pairs):
            sib_copy(step, c, lo).wait_send()
        return carry

    lax.fori_loop(0, chunks, drain, 0)


def per_device(members, owners, latent, w_message, edge_embed, w_node, w_output, send_list, edge_src, edge_feat, cell_area, target):
    nodes, width = latent.shape[1:]
    edges, points = edge_src.shape
    feats = edge_feat.shape[0]
    slots = send_list.shape[2]
    variables = w_output.shape[0]
    rows_in = owners * slots
    depth = rup(rows_in + 4 * feats, 128)
    chunks = points // CHUNK
    padded = rup(variables, 16)
    pairs = members // 2
    vmem = pl.BlockSpec(memory_space=pltpu.VMEM)
    hbm = pl.BlockSpec(memory_space=pl.ANY)
    dma = pltpu.SemaphoreType.DMA
    latent_grad, score = pl.pallas_call(
        functools.partial(kernel, members, owners),
        out_shape=(
            jax.ShapeDtypeStruct((1, nodes, width), BF16),
            jax.ShapeDtypeStruct((1, points), F32),
        ),
        in_specs=[vmem, hbm, vmem, hbm, vmem, vmem, vmem, vmem, vmem, vmem],
        out_specs=(vmem, vmem),
        scratch_shapes=[
            pltpu.VMEM((width, width), BF16),
            pltpu.VMEM((width, width), BF16),
            pltpu.VMEM((rows_in, nodes), F32),
            pltpu.VMEM((owners, slots, width), F32),
            pltpu.VMEM((owners, slots, width), F32),
            pltpu.VMEM((owners, slots, width), F32),
            pltpu.VMEM((owners, slots, width), F32),
            pltpu.VMEM((edges, rows_in, points), BF16),
            pltpu.VMEM((edges, points, depth), BF16),
            pltpu.VMEM((depth, width), BF16),
            pltpu.VMEM((16, 128), F32),
            pltpu.VMEM((CHUNK, width), BF16),
            pltpu.VMEM((CHUNK, width), BF16),
            pltpu.VMEM((edges, points, width), BF16),
            pltpu.VMEM((points, width), F32),
            pltpu.VMEM((CHUNK, width), F32),
            pltpu.VMEM((CHUNK, width), BF16),
            pltpu.VMEM((members, chunks, padded, CHUNK), BF16),
            pltpu.VMEM((rows_in, width), F32),
            dma((2,)),
            dma((owners,)),
            dma((owners,)),
            dma((owners,)),
            dma((owners,)),
            dma((pairs, chunks)),
            dma((pairs, chunks)),
            dma((pairs, chunks)),
            dma((pairs, chunks)),
        ],
        compiler_params=pltpu.CompilerParams(
            collective_id=0, has_side_effects=True, vmem_limit_bytes=48 * 1024 * 1024
        ),
    )(
        latent,
        w_message,
        edge_embed,
        w_node,
        w_output,
        send_list,
        edge_src,
        edge_feat,
        cell_area.reshape(1, points),
        target,
    )
    return latent_grad, score.reshape(points)


def solution(mesh):
    return jax.shard_map(
        functools.partial(per_device, mesh.shape["member"], mesh.shape["grid"]),
        mesh=mesh,
        in_specs=(
            P(("groups", "member"), "grid", None),
            P(),
            P(),
            P(),
            P(),
            P("grid", None, None),
            P(None, "grid"),
            P(None, None, "grid"),
            P("grid"),
            P(None, ("groups", "grid")),
        ),
        out_specs=(P(("groups", "member"), "grid", None), P(("groups", "grid"))),
        check_vma=False,
    )
```

```python
import functools

import jax
import jax.numpy as jnp
from jax import lax
from jax.experimental import pallas as pl
from jax.experimental.pallas import tpu as pltpu
from jax.sharding import PartitionSpec as P

F32 = jnp.float32
BF16 = jnp.bfloat16
MESH = pl.DeviceIdType.MESH

softness = 0.1
CHUNK = 512
TILE = 512


def rup(value, unit):
    return (value + unit - 1) // unit * unit


def fold(rows, owners):
    slots, width = rows.shape[0] // owners, rows.shape[1]
    split = rows.reshape(owners, slots, width)
    halves = [split[:, :, : width // 2], split[:, :, width // 2 :]]
    return jnp.concatenate(halves, axis=1).astype(BF16)


def unfold(blocks):
    wide = blocks.astype(F32)
    owners, slots, half = wide.shape[0], wide.shape[1] // 2, wide.shape[2]
    halves = [wide[:, :slots, :], wide[:, slots:, :]]
    return jnp.concatenate(halves, axis=2).reshape(owners * slots, 2 * half)


def tn_dot(a, b):
    return lax.dot_general(a, b, (((0,), (0,)), ((), ())), preferred_element_type=F32)


def nn_dot(a, b):
    return jnp.dot(a, b, preferred_element_type=F32)


def kernel(
    members,
    owners,
    latent_hbm,
    wm_hbm,
    embed_hbm,
    wn_hbm,
    wo_hbm,
    sends_hbm,
    src_hbm,
    feat_hbm,
    area_hbm,
    target_hbm,
    grad_ref,
    score_ref,
    latent_ref,
    wm,
    embed_ref,
    wn,
    wo_ref,
    sends_ref,
    src_ref,
    feat_ref,
    area_ref,
    target_ref,
    table,
    outgoing,
    received,
    back,
    returned,
    picks,
    picks_t,
    terms,
    hid,
    outr,
    edge_slope,
    mix_slope,
    go_scr,
    gm_scr,
    ens,
    slot,
    wn_t,
    wm_t,
    wo_wide,
    wo_t,
    local_sem,
    out_send,
    out_recv,
    back_send,
    back_recv,
    cross_send,
    cross_recv,
    sib_send,
    sib_recv,
):
    width = latent_ref.shape[2]
    nodes = latent_ref.shape[1]
    edges, points = src_ref.shape
    feats = feat_ref.shape[1]
    slots = sends_ref.shape[2]
    variables = wo_ref.shape[0]
    rows_in = owners * slots
    chunks = points // CHUNK
    tiles = [slice(t, t + TILE) for t in range(0, width, TILE)]
    pairs = members // 2

    zi = lax.axis_index("grid")
    mi = lax.axis_index("member")
    hi, lo = lax.div(mi, 2), lax.rem(mi, 2)
    sibling = hi * 2 + 1 - lo

    loads = [
        pltpu.make_async_copy(source, held, local_sem.at[which])
        for which, (source, held) in enumerate(
            [
                (sends_hbm, sends_ref),
                (latent_hbm, latent_ref),
                (wm_hbm, wm),
                (src_hbm, src_ref),
                (feat_hbm, feat_ref),
                (embed_hbm, embed_ref),
                (wn_hbm, wn),
                (wo_hbm, wo_ref),
                (area_hbm, area_ref),
                (target_hbm, target_ref),
            ]
        )
    ]
    for load in loads:
        load.start()

    def grid_peer(step):
        return lax.rem(zi + step, owners)

    def member_peer(step):
        return lax.rem(hi + step, pairs) * 2 + lo

    barrier = pltpu.get_barrier_semaphore()
    for step in range(1, owners):
        pl.semaphore_signal(
            barrier, inc=1, device_id={"grid": grid_peer(step)}, device_id_type=MESH
        )
    for step in range(1, pairs):
        pl.semaphore_signal(
            barrier, inc=1, device_id={"member": member_peer(step)}, device_id_type=MESH
        )
    pl.semaphore_signal(barrier, inc=1, device_id={"member": sibling}, device_id_type=MESH)

    loads[0].wait()
    eye = lax.broadcasted_iota(jnp.int32, (slots, slots), 0) == lax.broadcasted_iota(
        jnp.int32, (slots, slots), 1
    )
    node_id = lax.broadcasted_iota(jnp.int32, (slots, nodes), 1).astype(F32)
    for block in range(owners):
        line = jnp.broadcast_to(sends_ref[0, block : block + 1, :].astype(F32), (slots, slots))
        column = jnp.sum(jnp.where(eye, line, 0.0), axis=1, keepdims=True)
        table[block * slots : (block + 1) * slots, :] = jnp.where(column == node_id, 1.0, 0.0)

    loads[1].wait()
    outgoing[...] = fold(nn_dot(table[...].astype(BF16), latent_ref[0]), owners)

    pl.semaphore_wait(barrier, owners - 1 + pairs - 1 + 1)

    def out_copy(step):
        return pltpu.make_async_remote_copy(
            src_ref=outgoing.at[grid_peer(step)],
            dst_ref=received.at[zi],
            send_sem=out_send.at[step],
            recv_sem=out_recv.at[step],
            device_id={"grid": grid_peer(step)},
            device_id_type=MESH,
        )

    def out_arrival(step):
        origin = lax.rem(zi + owners - step, owners)
        return pltpu.make_async_remote_copy(
            src_ref=outgoing.at[origin],
            dst_ref=received.at[origin],
            send_sem=out_send.at[step],
            recv_sem=out_recv.at[step],
            device_id={"grid": origin},
            device_id_type=MESH,
        )

    for step in range(owners - 1, 0, -1):
        out_copy(step).start()
    received[zi] = outgoing[zi]

    for load in loads[3:6]:
        load.wait()
    depth = terms.shape[0]
    for edge in range(edges):
        slot_id = lax.broadcasted_iota(jnp.int32, (rows_in, points), 0)
        hot = jnp.where(slot_id == src_ref[edge : edge + 1, :], 1.0, 0.0)
        picks[edge] = hot.astype(BF16)
        value = feat_ref[edge]
        high = value.astype(BF16).astype(F32)
        rest = value - high
        parts = [hot, high, rest, high, rest]
        parts.append(jnp.zeros((depth - rows_in - 4 * feats, points), F32))
        picks_t[edge] = jnp.concatenate(parts, axis=0).T.astype(BF16)
    embed = embed_ref[...] * 0.5
    high = embed.astype(BF16).astype(F32)
    rest = embed - high
    tail = [high, high, rest, rest]
    tail.append(jnp.zeros((depth - rows_in - 4 * feats, width), F32))
    terms[rows_in:, :] = jnp.concatenate(tail, axis=0).astype(BF16)
    slot[...] = jnp.zeros(slot.shape, F32)
    for load in loads[6:]:
        load.wait()
    for tile in tiles:
        wn_t[:, tile] = wn[tile, :].T
    wo_wide[...] = jnp.zeros(wo_wide.shape, F32)
    wo_wide[:variables, :] = wo_ref[...].astype(F32)
    wo_t[...] = wo_wide[...].T.astype(BF16)
    loads[2].wait()

    for step in range(1, owners):
        out_arrival(step).wait_recv()
    projected = nn_dot(unfold(received[...]).astype(BF16), wm[...]).astype(BF16).astype(F32)
    terms[:rows_in, :] = (projected * 0.5).astype(BF16)
    for tile in tiles:
        wm_t[:, tile] = wm[tile, :].T

    def cross_copy(step, c):
        return pltpu.make_async_remote_copy(
            src_ref=ens.at[mi, c],
            dst_ref=ens.at[mi, c],
            send_sem=cross_send.at[step, c],
            recv_sem=cross_recv.at[step, c],
            device_id={"member": member_peer(step)},
            device_id_type=MESH,
        )

    def origin_of(step, side):
        return lax.rem(hi + pairs - step, pairs) * 2 + side

    def cross_arrival(step, c):
        origin = origin_of(step, lo)
        return pltpu.make_async_remote_copy(
            src_ref=ens.at[origin, c],
            dst_ref=ens.at[origin, c],
            send_sem=cross_send.at[step, c],
            recv_sem=cross_recv.at[step, c],
            device_id={"member": origin},
            device_id_type=MESH,
        )

    def sib_copy(step, c, side):
        held = ens.at[origin_of(step, side), c]
        return pltpu.make_async_remote_copy(
            src_ref=held,
            dst_ref=held,
            send_sem=sib_send.at[step, c],
            recv_sem=sib_recv.at[step, c],
            device_id={"member": sibling},
            device_id_type=MESH,
        )

    def pass_on(c):
        for step in range(1, pairs):
            cross_arrival(step, c).wait_recv()
            sib_copy(step, c, lo).start()

    def edge_tile(c, tile):
        span = pl.ds(pl.multiple_of(c * CHUNK, CHUNK), CHUNK)
        total = None
        for edge in range(edges):
            half = nn_dot(picks_t[edge, span, :], terms[:, tile])
            th = jnp.tanh(half)
            bent = half * th
            act = half + bent
            total = act if total is None else total + act
            edge_slope[edge, span, tile] = ((th + 1.0) + (half - bent * th)).astype(BF16)
        hid[0, :, tile] = (total * (1.0 / edges)).astype(BF16)

    def mix_tile(c, tile):
        span = pl.ds(pl.multiple_of(c * CHUNK, CHUNK), CHUNK)
        half = nn_dot(hid[0], wn[:, tile]) * 0.5
        th = jnp.tanh(half)
        bent = half * th
        mix_slope[span, tile] = ((th + 1.0) + (half - bent * th)) * 0.5
        outr[0, :, tile] = (hid[0, :, tile].astype(F32) + (half + bent)).astype(BF16)

    def forward(c, carry):
        for tile in tiles:
            edge_tile(c, tile)
        for tile in tiles:
            mix_tile(c, tile)
        guess = nn_dot(outr[0], wo_t[...]).T
        ens[mi, c] = guess[: ens.shape[2], :].astype(BF16)
        for step in range(1, pairs):
            cross_copy(step, c).start()
        sib_copy(0, c, lo).start()

        @pl.when(c > 0)
        def _():
            pass_on(c - 1)

        return carry

    lax.fori_loop(0, chunks, forward, 0)

    eps = softness * softness

    def lead(c):
        span = pl.ds(pl.multiple_of(c * CHUNK, CHUNK), CHUNK)
        for step in range(pairs):
            sib_copy(step, c, 1 - lo).wait_recv()
        own = ens[mi, c, :variables, :].astype(F32)
        spread = jnp.zeros(own.shape, F32)
        for member in range(members):
            gap = own - ens[member, c, :variables, :].astype(F32)
            spread = spread + gap * lax.rsqrt(gap * gap + eps)
        gap = own - target_ref[:, span].astype(F32)
        slope = gap * lax.rsqrt(gap * gap + eps) * (1.0 / members) - spread * (
            1.0 / (members * (members - 1))
        )
        return (area_ref[:, span] * slope).astype(BF16)

    def lead_tile(c, gp, tile):
        span = pl.ds(pl.multiple_of(c * CHUNK, CHUNK), CHUNK)
        go = tn_dot(gp, wo_ref[:, tile])
        go_scr[0, :, tile] = go
        gm_scr[0, :, tile] = (go * mix_slope[span, tile]).astype(BF16)

    def edge_back(c, tile):
        span = pl.ds(pl.multiple_of(c * CHUNK, CHUNK), CHUNK)
        gh = go_scr[0, :, tile] + nn_dot(gm_scr[0], wn_t[:, tile])
        gh = gh * (0.5 / edges)
        add = None
        for edge in range(edges):
            eg = (gh * edge_slope[edge, span, tile].astype(F32)).astype(BF16)
            part = nn_dot(picks[edge, :, span], eg)
            add = part if add is None else add + part
        slot[:, tile] += add

    def backward(c, carry):
        gp = lead(c)
        for tile in tiles:
            lead_tile(c, gp, tile)
        for tile in tiles:
            edge_back(c, tile)

        @pl.when(c == 0)
        def _():
            pass_on(chunks - 1)

        return carry

    lax.fori_loop(0, chunks, backward, 0)

    back[...] = fold(slot[...], owners)

    def back_copy(step):
        return pltpu.make_async_remote_copy(
            src_ref=back.at[grid_peer(step)],
            dst_ref=returned.at[zi],
            send_sem=back_send.at[step],
            recv_sem=back_recv.at[step],
            device_id={"grid": grid_peer(step)},
            device_id_type=MESH,
        )

    def back_arrival(step):
        origin = lax.rem(zi + owners - step, owners)
        return pltpu.make_async_remote_copy(
            src_ref=back.at[origin],
            dst_ref=returned.at[origin],
            send_sem=back_send.at[step],
            recv_sem=back_recv.at[step],
            device_id={"grid": origin},
            device_id_type=MESH,
        )

    for step in range(owners - 1, 0, -1):
        back_copy(step).start()
    returned[zi] = back[zi]

    def score(c, carry):
        span = pl.ds(pl.multiple_of(c * CHUNK, CHUNK), CHUNK)
        truth = target_ref[:, span].astype(F32)
        values = [ens[member, c, :variables, :].astype(F32) for member in range(members)]
        skill = jnp.zeros(truth.shape, F32)
        spread = jnp.zeros(truth.shape, F32)
        for a in range(members):
            gap = values[a] - truth
            gap = gap * gap + eps
            skill = skill + gap * lax.rsqrt(gap)
            for b in range(a):
                gap = values[a] - values[b]
                gap = gap * gap + eps
                spread = spread + gap * lax.rsqrt(gap)
        crps = skill * (1.0 / members) - spread * (1.0 / (members * (members - 1)))
        mean = jnp.sum(crps, axis=0, keepdims=True) * (1.0 / variables)
        score_ref[:, span] = area_ref[:, span] * mean
        return carry

    lax.fori_loop(0, chunks, score, 0)

    for step in range(1, owners):
        back_arrival(step).wait_recv()
    gathered = unfold(returned[...]).astype(BF16)
    row_grad = tn_dot(table[...].astype(BF16), gathered).astype(BF16)
    grad_ref[0] = nn_dot(row_grad, wm_t[...]).astype(BF16)

    for step in range(1, owners):
        out_copy(step).wait_send()
        back_copy(step).wait_send()

    def drain(c, carry):
        for step in range(1, pairs):
            cross_copy(step, c).wait_send()
        for step in range(pairs):
            sib_copy(step, c, lo).wait_send()
        return carry

    lax.fori_loop(0, chunks, drain, 0)


def per_device(members, owners, latent, w_message, edge_embed, w_node, w_output, send_list, edge_src, edge_feat, cell_area, target):
    nodes, width = latent.shape[1:]
    edges, points = edge_src.shape
    feats = edge_feat.shape[0]
    edge_feat = jnp.transpose(edge_feat, (1, 0, 2))
    cell_area = cell_area.reshape(1, points)
    slots = send_list.shape[2]
    variables = w_output.shape[0]
    rows_in = owners * slots
    depth = rup(rows_in + 4 * feats, 128)
    chunks = points // CHUNK
    padded = rup(variables, 16)
    pairs = members // 2
    arrays = (
        latent,
        w_message,
        edge_embed,
        w_node,
        w_output,
        send_list,
        edge_src,
        edge_feat,
        cell_area,
        target,
    )
    vmem = pl.BlockSpec(memory_space=pltpu.VMEM)
    hbm = pl.BlockSpec(memory_space=pltpu.HBM)
    dma = pltpu.SemaphoreType.DMA
    latent_grad, score = pl.pallas_call(
        functools.partial(kernel, members, owners),
        out_shape=(
            pltpu.VMEM((1, nodes, width), BF16),
            pltpu.VMEM((1, points), F32),
        ),
        in_specs=[hbm] * 10,
        out_specs=(vmem, vmem),
        scratch_shapes=[
            *[pltpu.VMEM(array.shape, array.dtype) for array in arrays],
            pltpu.VMEM((rows_in, nodes), F32),
            pltpu.VMEM((owners, 2 * slots, width // 2), BF16),
            pltpu.VMEM((owners, 2 * slots, width // 2), BF16),
            pltpu.VMEM((owners, 2 * slots, width // 2), BF16),
            pltpu.VMEM((owners, 2 * slots, width // 2), BF16),
            pltpu.VMEM((edges, rows_in, points), BF16),
            pltpu.VMEM((edges, points, depth), BF16),
            pltpu.VMEM((depth, width), BF16),
            pltpu.VMEM((2, CHUNK, width), BF16),
            pltpu.VMEM((2, CHUNK, width), BF16),
            pltpu.VMEM((edges, points, width), BF16),
            pltpu.VMEM((points, width), F32),
            pltpu.VMEM((2, CHUNK, width), F32),
            pltpu.VMEM((2, CHUNK, width), BF16),
            pltpu.VMEM((members, chunks, padded, CHUNK), BF16),
            pltpu.VMEM((rows_in, width), F32),
            pltpu.VMEM((width, width), BF16),
            pltpu.VMEM((width, width), BF16),
            pltpu.VMEM((rup(variables, 128), width), F32),
            pltpu.VMEM((width, rup(variables, 128)), BF16),
            dma((len(arrays),)),
            dma((owners,)),
            dma((owners,)),
            dma((owners,)),
            dma((owners,)),
            dma((pairs, chunks)),
            dma((pairs, chunks)),
            dma((pairs, chunks)),
            dma((pairs, chunks)),
        ],
        compiler_params=pltpu.CompilerParams(
            collective_id=0, has_side_effects=True, vmem_limit_bytes=60 * 1024 * 1024
        ),
    )(*arrays)
    return latent_grad, score.reshape(points)


def solution(mesh):
    return jax.shard_map(
        functools.partial(per_device, mesh.shape["member"], mesh.shape["grid"]),
        mesh=mesh,
        in_specs=(
            P(("groups", "member"), "grid", None),
            P(),
            P(),
            P(),
            P(),
            P("grid", None, None),
            P(None, "grid"),
            P(None, None, "grid"),
            P("grid"),
            P(None, ("groups", "grid")),
        ),
        out_specs=(P(("groups", "member"), "grid", None), P(("groups", "grid"))),
        check_vma=False,
    )
```

```python
import functools

import jax
import jax.numpy as jnp
from jax import lax
from jax.experimental import pallas as pl
from jax.experimental.pallas import tpu as pltpu
from jax.sharding import PartitionSpec as P

F32 = jnp.float32
BF16 = jnp.bfloat16
MESH = pl.DeviceIdType.MESH

softness = 0.1
CHUNK = 512
TILE = 512
NARROW = 128


def rup(value, unit):
    return (value + unit - 1) // unit * unit


def fold(rows, owners):
    slots, width = rows.shape[0] // owners, rows.shape[1]
    split = rows.reshape(owners, slots, width)
    halves = [split[:, :, : width // 2], split[:, :, width // 2 :]]
    return jnp.concatenate(halves, axis=1).astype(BF16)


def unfold(blocks):
    wide = blocks.astype(F32)
    owners, slots, half = wide.shape[0], wide.shape[1] // 2, wide.shape[2]
    halves = [wide[:, :slots, :], wide[:, slots:, :]]
    return jnp.concatenate(halves, axis=2).reshape(owners * slots, 2 * half)


def tn_dot(a, b):
    return lax.dot_general(a, b, (((0,), (0,)), ((), ())), preferred_element_type=F32)


def nn_dot(a, b):
    return jnp.dot(a, b, preferred_element_type=F32)


def kernel(
    members,
    owners,
    latent_hbm,
    wm_hbm,
    embed_hbm,
    wn_hbm,
    wo_hbm,
    sends_hbm,
    src_hbm,
    feat_hbm,
    area_hbm,
    target_hbm,
    grad_ref,
    score_ref,
    latent_ref,
    wm,
    embed_ref,
    wn,
    wo_ref,
    sends_ref,
    src_ref,
    feat_ref,
    area_ref,
    target_ref,
    table,
    outgoing,
    received,
    back,
    returned,
    picks,
    picks_t,
    terms,
    hid,
    outr,
    edge_slope,
    mix_slope,
    go_scr,
    gm_scr,
    ens,
    slot,
    wn_t,
    wm_t,
    wo_wide,
    wo_t,
    local_sem,
    out_send,
    out_recv,
    back_send,
    back_recv,
    cross_send,
    cross_recv,
    sib_send,
    sib_recv,
):
    width = latent_ref.shape[2]
    nodes = latent_ref.shape[1]
    edges, points = src_ref.shape
    feats = feat_ref.shape[1]
    slots = sends_ref.shape[2]
    variables = wo_ref.shape[0]
    rows_in = owners * slots
    chunks = points // CHUNK
    tiles = [slice(t, t + TILE) for t in range(0, width, TILE)]
    pairs = members // 2

    zi = lax.axis_index("grid")
    mi = lax.axis_index("member")
    hi, lo = lax.div(mi, 2), lax.rem(mi, 2)
    sibling = hi * 2 + 1 - lo

    loads = [
        pltpu.make_async_copy(source, held, local_sem.at[which])
        for which, (source, held) in enumerate(
            [
                (sends_hbm, sends_ref),
                (latent_hbm, latent_ref),
                (wm_hbm, wm),
                (src_hbm, src_ref),
                (feat_hbm, feat_ref),
                (embed_hbm, embed_ref),
                (wn_hbm, wn),
                (wo_hbm, wo_ref),
                (area_hbm, area_ref),
                (target_hbm, target_ref),
            ]
        )
    ]
    for load in loads:
        load.start()

    def grid_peer(step):
        return lax.rem(zi + step, owners)

    def member_peer(step):
        return lax.rem(hi + step, pairs) * 2 + lo

    barrier = pltpu.get_barrier_semaphore()
    for step in range(1, owners):
        pl.semaphore_signal(
            barrier, inc=1, device_id={"grid": grid_peer(step)}, device_id_type=MESH
        )
    for step in range(1, pairs):
        pl.semaphore_signal(
            barrier, inc=1, device_id={"member": member_peer(step)}, device_id_type=MESH
        )
    pl.semaphore_signal(barrier, inc=1, device_id={"member": sibling}, device_id_type=MESH)

    loads[0].wait()
    eye = lax.broadcasted_iota(jnp.int32, (slots, slots), 0) == lax.broadcasted_iota(
        jnp.int32, (slots, slots), 1
    )
    node_id = lax.broadcasted_iota(jnp.int32, (slots, nodes), 1).astype(F32)
    for block in range(owners):
        line = jnp.broadcast_to(sends_ref[0, block : block + 1, :].astype(F32), (slots, slots))
        column = jnp.sum(jnp.where(eye, line, 0.0), axis=1, keepdims=True)
        table[block * slots : (block + 1) * slots, :] = jnp.where(column == node_id, 1.0, 0.0)

    loads[1].wait()
    outgoing[...] = fold(nn_dot(table[...].astype(BF16), latent_ref[0]), owners)

    pl.semaphore_wait(barrier, owners - 1 + pairs - 1 + 1)

    def out_copy(step):
        return pltpu.make_async_remote_copy(
            src_ref=outgoing.at[grid_peer(step)],
            dst_ref=received.at[zi],
            send_sem=out_send.at[step],
            recv_sem=out_recv.at[step],
            device_id={"grid": grid_peer(step)},
            device_id_type=MESH,
        )

    def out_arrival(step):
        origin = lax.rem(zi + owners - step, owners)
        return pltpu.make_async_remote_copy(
            src_ref=outgoing.at[origin],
            dst_ref=received.at[origin],
            send_sem=out_send.at[step],
            recv_sem=out_recv.at[step],
            device_id={"grid": origin},
            device_id_type=MESH,
        )

    for step in range(owners - 1, 0, -1):
        out_copy(step).start()
    received[zi] = outgoing[zi]

    for load in loads[3:6]:
        load.wait()
    depth = terms.shape[0]
    for edge in range(edges):
        slot_id = lax.broadcasted_iota(jnp.int32, (rows_in, points), 0)
        hot = jnp.where(slot_id == src_ref[edge : edge + 1, :], 1.0, 0.0)
        picks[edge] = hot.astype(BF16)
        value = feat_ref[edge]
        high = value.astype(BF16).astype(F32)
        rest = value - high
        parts = [hot, high, rest, high, rest]
        parts.append(jnp.zeros((depth - rows_in - 4 * feats, points), F32))
        picks_t[edge] = jnp.concatenate(parts, axis=0).T.astype(BF16)
    embed = embed_ref[...] * 0.5
    high = embed.astype(BF16).astype(F32)
    rest = embed - high
    tail = [high, high, rest, rest]
    tail.append(jnp.zeros((depth - rows_in - 4 * feats, width), F32))
    terms[rows_in:, :] = jnp.concatenate(tail, axis=0).astype(BF16)
    slot[...] = jnp.zeros(slot.shape, F32)
    for load in loads[6:]:
        load.wait()
    for tile in tiles:
        wn_t[:, tile] = wn[tile, :].T
    wo_wide[...] = jnp.zeros(wo_wide.shape, F32)
    wo_wide[:variables, :] = wo_ref[...].astype(F32)
    wo_t[...] = wo_wide[...].T.astype(BF16)
    loads[2].wait()

    for step in range(1, owners):
        out_arrival(step).wait_recv()
    projected = nn_dot(unfold(received[...]).astype(BF16), wm[...]).astype(BF16).astype(F32)
    terms[:rows_in, :] = (projected * 0.5).astype(BF16)

    def cross_copy(step, c):
        return pltpu.make_async_remote_copy(
            src_ref=ens.at[mi, c],
            dst_ref=ens.at[mi, c],
            send_sem=cross_send.at[step, c],
            recv_sem=cross_recv.at[step, c],
            device_id={"member": member_peer(step)},
            device_id_type=MESH,
        )

    def origin_of(step, side):
        return lax.rem(hi + pairs - step, pairs) * 2 + side

    def cross_arrival(step, c):
        origin = origin_of(step, lo)
        return pltpu.make_async_remote_copy(
            src_ref=ens.at[origin, c],
            dst_ref=ens.at[origin, c],
            send_sem=cross_send.at[step, c],
            recv_sem=cross_recv.at[step, c],
            device_id={"member": origin},
            device_id_type=MESH,
        )

    def sib_copy(step, c, side):
        held = ens.at[origin_of(step, side), c]
        return pltpu.make_async_remote_copy(
            src_ref=held,
            dst_ref=held,
            send_sem=sib_send.at[step, c],
            recv_sem=sib_recv.at[step, c],
            device_id={"member": sibling},
            device_id_type=MESH,
        )

    def pass_on(c):
        for step in range(1, pairs):
            cross_arrival(step, c).wait_recv()
            sib_copy(step, c, lo).start()

    def edge_tile(c, tile):
        span = pl.ds(pl.multiple_of(c * CHUNK, CHUNK), CHUNK)
        total = None
        for edge in range(edges):
            half = nn_dot(picks_t[edge, span, :], terms[:, tile])
            th = jnp.tanh(half)
            bent = half * th
            act = half + bent
            total = act if total is None else total + act
            edge_slope[edge, span, tile] = ((th + 1.0) + (half - bent * th)).astype(BF16)
        hid[0, :, tile] = (total * (1.0 / edges)).astype(BF16)

    def mix_tile(c, tile):
        span = pl.ds(pl.multiple_of(c * CHUNK, CHUNK), CHUNK)
        half = nn_dot(hid[0], wn[:, tile]) * 0.5
        th = jnp.tanh(half)
        bent = half * th
        mix_slope[span, tile] = ((th + 1.0) + (half - bent * th)) * 0.5
        outr[0, :, tile] = (hid[0, :, tile].astype(F32) + (half + bent)).astype(BF16)

    def forward(c, carry):
        for tile in tiles:
            edge_tile(c, tile)
        for tile in tiles:
            mix_tile(c, tile)
        guess = nn_dot(outr[0], wo_t[...]).T
        ens[mi, c] = guess[: ens.shape[2], :].astype(BF16)
        for step in range(1, pairs):
            cross_copy(step, c).start()
        sib_copy(0, c, lo).start()

        @pl.when(c > 0)
        def _():
            pass_on(c - 1)

        return carry

    lax.fori_loop(0, chunks, forward, 0)

    eps = softness * softness

    def lead(c):
        span = pl.ds(pl.multiple_of(c * CHUNK, CHUNK), CHUNK)
        for step in range(pairs):
            sib_copy(step, c, 1 - lo).wait_recv()
        own = ens[mi, c, :variables, :].astype(F32)
        spread = jnp.zeros(own.shape, F32)
        for member in range(members):
            gap = own - ens[member, c, :variables, :].astype(F32)
            spread = spread + gap * lax.rsqrt(gap * gap + eps)
        gap = own - target_ref[:, span].astype(F32)
        slope = gap * lax.rsqrt(gap * gap + eps) * (1.0 / members) - spread * (
            1.0 / (members * (members - 1))
        )
        return (area_ref[:, span] * slope).astype(BF16)

    def lead_tile(c, gp, tile):
        span = pl.ds(pl.multiple_of(c * CHUNK, CHUNK), CHUNK)
        go = tn_dot(gp, wo_ref[:, tile])
        go_scr[0, :, tile] = go
        gm_scr[0, :, tile] = (go * mix_slope[span, tile]).astype(BF16)

    def edge_back(c, tile):
        span = pl.ds(pl.multiple_of(c * CHUNK, CHUNK), CHUNK)
        gh = go_scr[0, :, tile] + nn_dot(gm_scr[0], wn_t[:, tile])
        gh = gh * (0.5 / edges)
        add = None
        for edge in range(edges):
            eg = (gh * edge_slope[edge, span, tile].astype(F32)).astype(BF16)
            part = nn_dot(picks[edge, :, span], eg)
            add = part if add is None else add + part
        slot[:, tile] += add

    def backward(c, carry):
        gp = lead(c)
        for tile in tiles:
            lead_tile(c, gp, tile)
        for tile in tiles:
            edge_back(c, tile)

        @pl.when(c == 0)
        def _():
            pass_on(chunks - 1)

        return carry

    lax.fori_loop(0, chunks, backward, 0)

    back[...] = fold(slot[...], owners)

    def back_copy(step):
        return pltpu.make_async_remote_copy(
            src_ref=back.at[grid_peer(step)],
            dst_ref=returned.at[zi],
            send_sem=back_send.at[step],
            recv_sem=back_recv.at[step],
            device_id={"grid": grid_peer(step)},
            device_id_type=MESH,
        )

    def back_arrival(step):
        origin = lax.rem(zi + owners - step, owners)
        return pltpu.make_async_remote_copy(
            src_ref=back.at[origin],
            dst_ref=returned.at[origin],
            send_sem=back_send.at[step],
            recv_sem=back_recv.at[step],
            device_id={"grid": origin},
            device_id_type=MESH,
        )

    for step in range(owners - 1, 0, -1):
        back_copy(step).start()
    returned[zi] = back[zi]

    def score(c, carry):
        span = pl.ds(pl.multiple_of(c * NARROW, NARROW), NARROW)
        held = lax.div(c, CHUNK // NARROW)
        part = pl.ds(pl.multiple_of(lax.rem(c, CHUNK // NARROW) * NARROW, NARROW), NARROW)
        truth = target_ref[:, span].astype(F32)
        values = [ens[member, held, :variables, part].astype(F32) for member in range(members)]
        skill = jnp.zeros(truth.shape, F32)
        spread = jnp.zeros(truth.shape, F32)
        for a in range(members):
            gap = values[a] - truth
            gap = gap * gap + eps
            skill = skill + gap * lax.rsqrt(gap)
            for b in range(a):
                gap = values[a] - values[b]
                gap = gap * gap + eps
                spread = spread + gap * lax.rsqrt(gap)
        crps = skill * (1.0 / members) - spread * (1.0 / (members * (members - 1)))
        mean = jnp.sum(crps, axis=0, keepdims=True) * (1.0 / variables)
        score_ref[:, span] = area_ref[:, span] * mean
        return carry

    for tile in tiles:
        wm_t[:, tile] = wm[tile, :].T
    lax.fori_loop(0, points // NARROW, score, 0)

    for step in range(1, owners):
        back_arrival(step).wait_recv()
    gathered = unfold(returned[...]).astype(BF16)
    row_grad = tn_dot(table[...].astype(BF16), gathered).astype(BF16)
    grad_ref[0] = nn_dot(row_grad, wm_t[...]).astype(BF16)

    for step in range(1, owners):
        out_copy(step).wait_send()
        back_copy(step).wait_send()

    def drain(c, carry):
        for step in range(1, pairs):
            cross_copy(step, c).wait_send()
        for step in range(pairs):
            sib_copy(step, c, lo).wait_send()
        return carry

    lax.fori_loop(0, chunks, drain, 0)


def per_device(members, owners, latent, w_message, edge_embed, w_node, w_output, send_list, edge_src, edge_feat, cell_area, target):
    nodes, width = latent.shape[1:]
    edges, points = edge_src.shape
    feats = edge_feat.shape[0]
    edge_feat = jnp.transpose(edge_feat, (1, 0, 2))
    cell_area = cell_area.reshape(1, points)
    slots = send_list.shape[2]
    variables = w_output.shape[0]
    rows_in = owners * slots
    depth = rup(rows_in + 4 * feats, 128)
    chunks = points // CHUNK
    padded = rup(variables, 16)
    pairs = members // 2
    arrays = (
        latent,
        w_message,
        edge_embed,
        w_node,
        w_output,
        send_list,
        edge_src,
        edge_feat,
        cell_area,
        target,
    )
    vmem = pl.BlockSpec(memory_space=pltpu.VMEM)
    hbm = pl.BlockSpec(memory_space=pltpu.HBM)
    dma = pltpu.SemaphoreType.DMA
    latent_grad, score = pl.pallas_call(
        functools.partial(kernel, members, owners),
        out_shape=(
            pltpu.VMEM((1, nodes, width), BF16),
            pltpu.VMEM((1, points), F32),
        ),
        in_specs=[hbm] * 10,
        out_specs=(vmem, vmem),
        scratch_shapes=[
            *[pltpu.VMEM(array.shape, array.dtype) for array in arrays],
            pltpu.VMEM((rows_in, nodes), F32),
            pltpu.VMEM((owners, 2 * slots, width // 2), BF16),
            pltpu.VMEM((owners, 2 * slots, width // 2), BF16),
            pltpu.VMEM((owners, 2 * slots, width // 2), BF16),
            pltpu.VMEM((owners, 2 * slots, width // 2), BF16),
            pltpu.VMEM((edges, rows_in, points), BF16),
            pltpu.VMEM((edges, points, depth), BF16),
            pltpu.VMEM((depth, width), BF16),
            pltpu.VMEM((2, CHUNK, width), BF16),
            pltpu.VMEM((2, CHUNK, width), BF16),
            pltpu.VMEM((edges, points, width), BF16),
            pltpu.VMEM((points, width), F32),
            pltpu.VMEM((2, CHUNK, width), F32),
            pltpu.VMEM((2, CHUNK, width), BF16),
            pltpu.VMEM((members, chunks, padded, CHUNK), BF16),
            pltpu.VMEM((rows_in, width), F32),
            pltpu.VMEM((width, width), BF16),
            pltpu.VMEM((width, width), BF16),
            pltpu.VMEM((rup(variables, 128), width), F32),
            pltpu.VMEM((width, rup(variables, 128)), BF16),
            dma((len(arrays),)),
            dma((owners,)),
            dma((owners,)),
            dma((owners,)),
            dma((owners,)),
            dma((pairs, chunks)),
            dma((pairs, chunks)),
            dma((pairs, chunks)),
            dma((pairs, chunks)),
        ],
        compiler_params=pltpu.CompilerParams(
            collective_id=0, has_side_effects=True, vmem_limit_bytes=60 * 1024 * 1024
        ),
    )(*arrays)
    return latent_grad, score.reshape(points)


def solution(mesh):
    return jax.shard_map(
        functools.partial(per_device, mesh.shape["member"], mesh.shape["grid"]),
        mesh=mesh,
        in_specs=(
            P(("groups", "member"), "grid", None),
            P(),
            P(),
            P(),
            P(),
            P("grid", None, None),
            P(None, "grid"),
            P(None, None, "grid"),
            P("grid"),
            P(None, ("groups", "grid")),
        ),
        out_specs=(P(("groups", "member"), "grid", None), P(("groups", "grid"))),
        check_vma=False,
    )
```
